256 devices in a mesh: dp: 32 (over z, y), ctx: 8 (over x, core).
Axes of the slice: x: 4, y: 4, z: 8, core: 2. Of those that a mesh axis runs over, the one named last changes fastest.
Arguments:
- queries: bfloat16 [32, 1024, 8192], P('dp', 'ctx'), may hold values from -100 to 100
- keys: bfloat16 [32, 1024, 1024], P('dp', 'ctx'), may hold values from -8 to 8
- values: bfloat16 [32, 1024, 1024], P('dp', 'ctx'), may hold values from -6 to 6
- upstream: bfloat16 [32, 1024, 8192], P('dp', 'ctx'), may hold values from -0.6 to 0.6
- token_logp: float32 [32, 1024], P('dp', 'ctx'), may hold values from -4 to -0.05
- segments: int32 [32, 1024], replicated, may hold values from 0 to 3, as said below
- partner: int32 [128], replicated, may hold values from 0 to 127, as said below
- chosen: int32 [128], replicated, may hold values from 0 to 1, as said below
- ref_score: float32 [128], replicated, may hold values from -1 to 1
Outputs:
- grad_q: bfloat16 [32, 1024, 8192], P('dp', 'ctx')
- grad_k: bfloat16 [32, 1024, 1024], P('dp', 'ctx')
- grad_v: bfloat16 [32, 1024, 1024], P('dp', 'ctx')
- loss: float32 [], replicated
The draws below stay inside these ranges and needn't reach their ends.
Inputs may be any that keep to these rules, and one draw needn't show every extreme that they name: `segments`: segment numbers never fall along a pack and each of the 4 numbers appears in every pack; in every pack one sequence has exactly 512 tokens and every other one at least (512) // 6. partner[partner[g]] = g and partner[g] != g; every sequence lies in exactly one pair. `chosen`: exactly one sequence of each pair has 1.
All inputs are finite; a program needn't handle non-finite values.
Results may differ from the reference program's by a relative error of at most 0.022.
Values may be sent and summed in bfloat16 or wider, within the bound.
No kernel may reach another device: no remote copies, remote signals or barrier semaphores. Data moves between devices by JAX's collectives and lax.ppermute only.
A program may use at most 128 MiB of HBM per device.

```python
import jax
import jax.numpy as jnp
from jax import lax

H = 64
KV = 8
HD = 128
SEQS = 4
PACK = 1024
MOST = 512
N_DP = 32


def shared_keys(key):
    return jax.random.normal(key, (N_DP, PACK, KV * HD), jnp.float32)


def pair_order(key):
    return jax.random.permutation(key, N_DP * SEQS).astype(jnp.int32)


def pack_lengths(key):
    long_key, cut_key = jax.random.split(key)
    least_len = (PACK - MOST) // (2 * (SEQS - 1))
    spare_len = PACK - MOST - (SEQS - 1) * least_len
    cuts = jnp.sort(jax.random.randint(cut_key, (N_DP, SEQS - 2), 0, spare_len + 1).astype(jnp.int32), axis=1)
    edges = jnp.concatenate([jnp.zeros((N_DP, 1), jnp.int32), cuts, jnp.full((N_DP, 1), spare_len, jnp.int32)], axis=1)
    other_lens = least_len + edges[:, 1:] - edges[:, :-1]
    longest = jax.random.randint(long_key, (N_DP, 1), 0, SEQS).astype(jnp.int32)
    slot_ids = jnp.arange(SEQS, dtype=jnp.int32)[None, :]
    picked = jnp.clip(slot_ids - (slot_ids > longest).astype(jnp.int32), 0, SEQS - 2)
    return jnp.where(slot_ids == longest, MOST, jnp.take_along_axis(other_lens, picked, axis=1)).astype(jnp.int32)


def token_layout(lengths):
    ends = jnp.cumsum(lengths, axis=1).astype(jnp.int32)
    places = jnp.arange(PACK, dtype=jnp.int32)
    seq_index = jnp.sum((places[None, :, None] >= ends[:, None, :SEQS - 1]).astype(jnp.int32), axis=-1)
    return seq_index.astype(jnp.int32)


def draw_keys(key, part):
    base = shared_keys(key)
    base = jnp.clip(base, -6.0, 6.0)
    return jnp.clip(base, -8.0, 8.0).astype(jnp.bfloat16)


def draw_queries(key, part):
    key = jax.random.fold_in(key, 12)
    fresh = jnp.clip(jax.random.normal(key, (N_DP, PACK, H * HD), jnp.float32), -6.0, 6.0)
    return jnp.clip(fresh, -100.0, 100.0).astype(jnp.bfloat16)


def draw_segments(key, part):
    lengths = pack_lengths(key)
    seq_index = token_layout(lengths)
    return seq_index


def draw_upstream(key, part):
    key = jax.random.fold_in(key, 32)
    noise = jnp.clip(jax.random.normal(key, (N_DP, PACK, H * HD), jnp.float32), -6.0, 6.0)
    noise = noise * 0.05
    return noise.astype(jnp.bfloat16)


def draw_token_logp(key, part):
    key = jax.random.fold_in(key, 33)
    return jax.random.uniform(key, (N_DP, PACK), jnp.float32, -4.0, -0.05)


def draw_ref_score(key, part):
    key = jax.random.fold_in(key, 34)
    return jnp.clip(0.3 * jax.random.normal(key, (N_DP * SEQS,), jnp.float32), -1.0, 1.0)


def draw_partner(key, part):
    order = pair_order(key)
    mates = order.reshape(-1, 2)[:, ::-1].reshape(-1)
    return jnp.zeros((N_DP * SEQS,), jnp.int32).at[order].set(mates)


def draw_chosen(key, part):
    order = pair_order(key)
    flags = (jnp.arange(N_DP * SEQS) % 2 == 0).astype(jnp.int32)
    return jnp.zeros((N_DP * SEQS,), jnp.int32).at[order].set(flags)


def shard_levels(stream_key, shape, cuts, low, high):
    factor_of, own = 1.0, jax.random.fold_in(stream_key, 6)
    for axis_at, parts in cuts:
        steps = jnp.exp(jax.random.uniform(jax.random.fold_in(own, axis_at), (parts,), jnp.float32, low / len(cuts), high / len(cuts)))
        factor_of = factor_of * jnp.repeat(steps, shape[axis_at] // parts).reshape([-1 if axis == axis_at else 1 for axis in range(len(shape))])
    return factor_of


def bell_draw(rng, dims, scale, reach, pieces=(), held_as=jnp.bfloat16):
    entries = jax.random.normal(rng, dims, jnp.float32) * scale
    if len(pieces) > 0:
        entries = shard_levels(rng, dims, pieces, -0.22, 0.18) * entries
    return jnp.clip(entries, min=-reach, max=reach).astype(held_as)


def setup_inputs(seed: int = 0) -> dict:
    key_of = jax.random.split(jax.random.key(seed), 10)
    return {
        "queries": draw_queries(jax.random.fold_in(key_of[9], 71), 0),
        "keys": draw_keys(jax.random.fold_in(key_of[9], 71), 0),
        "values": bell_draw(key_of[2], (N_DP, PACK, KV * HD), 1.0, 6.0, ((0, 32), (1, 8))),
        "upstream": draw_upstream(jax.random.fold_in(key_of[9], 71), 0),
        "token_logp": draw_token_logp(jax.random.fold_in(key_of[9], 71), 0),
        "segments": draw_segments(jax.random.fold_in(key_of[9], 71), 0),
        "partner": draw_partner(jax.random.fold_in(key_of[9], 71), 0),
        "chosen": draw_chosen(jax.random.fold_in(key_of[9], 71), 0),
        "ref_score": draw_ref_score(jax.random.fold_in(key_of[9], 71), 0),
    }


NEG_FILL = -1e30
BETA = 2.0
LOSS_SCALE = 1024.0


def pack_mask(seg):
    pos = jnp.arange(seg.shape[0], dtype=jnp.int32)
    return (pos[None, :] <= pos[:, None]) & (seg[None, :] == seg[:, None])


def group_forward(q_group, k_head, v_head, allowed, scale):
    scores = jnp.einsum("qgd,sd->gqs", q_group.astype(jnp.float32), k_head.astype(jnp.float32)) * scale
    scores = jnp.where(allowed[None], scores, NEG_FILL)
    peak = jnp.max(scores, axis=-1, keepdims=True)
    expo = jnp.exp(scores - peak)
    weights = (expo / jnp.sum(expo, axis=-1, keepdims=True)).astype(jnp.bfloat16)
    out = jnp.einsum("gqs,sd->qgd", weights.astype(jnp.float32), v_head.astype(jnp.float32))
    return weights, out


def split_pack(q, k, v, u):
    group = H // KV
    return (q.reshape(PACK, KV, group, HD).transpose(1, 0, 2, 3),
            k.reshape(PACK, KV, HD).transpose(1, 0, 2),
            v.reshape(PACK, KV, HD).transpose(1, 0, 2),
            u.reshape(PACK, KV, group, HD).transpose(1, 0, 2, 3))


def reference(queries, keys, values, upstream, token_logp, segments, partner, chosen, ref_score):
    scale = HD ** -0.5
    slots = jnp.arange(SEQS, dtype=jnp.int32)

    def pack_terms(inputs):
        q, k, v, u, seg = inputs
        allowed = pack_mask(seg)
        q_all, k_all, v_all, u_all = split_pack(q, k, v, u)

        def one_head(items):
            q_head, k_head, v_head, u_head = items
            weights, out = group_forward(q_head, k_head, v_head, allowed, scale)
            return jnp.sum(out * u_head.astype(jnp.float32), axis=(1, 2))

        return jnp.sum(lax.map(one_head, (q_all, k_all, v_all, u_all)), axis=0)

    terms = lax.map(pack_terms, (queries, keys, values, upstream, segments))
    tokens = token_logp + terms
    onehot = (segments[:, :, None] == slots[None, None, :]).astype(jnp.float32)
    sums = jnp.sum(tokens[:, :, None] * onehot, axis=1).reshape(-1)
    lengths = jnp.sum(onehot, axis=1).reshape(-1)
    adjusted = sums / lengths - ref_score
    sign = 2.0 * chosen.astype(jnp.float32) - 1.0
    margin = BETA * sign * (adjusted - adjusted[partner])
    loss = jnp.sum(chosen.astype(jnp.float32) * jax.nn.softplus(-margin))
    weight = -sign * BETA * jax.nn.sigmoid(-margin) * LOSS_SCALE / lengths
    token_weight = jnp.sum(onehot * weight.reshape(N_DP, SEQS)[:, None, :], axis=-1)

    def pack_grads(inputs):
        q, k, v, u, seg, tw = inputs
        allowed = pack_mask(seg)
        q_all, k_all, v_all, u_all = split_pack(q, k, v, u)

        def one_head(items):
            q_head, k_head, v_head, u_head = items
            weights, out = group_forward(q_head, k_head, v_head, allowed, scale)
            dout = (tw[:, None, None] * u_head.astype(jnp.float32)).astype(jnp.bfloat16)
            dout_wide = dout.astype(jnp.float32)
            weights_wide = weights.astype(jnp.float32)
            value_grad = jnp.einsum("gqs,qgd->sd", weights_wide, dout_wide)
            dprob = jnp.einsum("qgd,sd->gqs", dout_wide, v_head.astype(jnp.float32))
            delta = jnp.sum(dout_wide * out, axis=-1).T[..., None]
            dscore = (weights_wide * (dprob - delta) * scale).astype(jnp.bfloat16)
            dscore_wide = dscore.astype(jnp.float32)
            query_grad = jnp.einsum("gqs,sd->qgd", dscore_wide, k_head.astype(jnp.float32))
            key_grad = jnp.einsum("gqs,qgd->sd", dscore_wide, q_head.astype(jnp.float32))
            return query_grad.astype(jnp.bfloat16), key_grad.astype(jnp.bfloat16), value_grad.astype(jnp.bfloat16)

        dq, dk, dv = lax.map(one_head, (q_all, k_all, v_all, u_all))
        return (dq.transpose(1, 0, 2, 3).reshape(PACK, H * HD),
                dk.transpose(1, 0, 2).reshape(PACK, KV * HD),
                dv.transpose(1, 0, 2).reshape(PACK, KV * HD))

    grad_q, grad_k, grad_v = lax.map(pack_grads, (queries, keys, values, upstream, segments, token_weight))
    return grad_q, grad_k, grad_v, loss
```

```python
import functools

import jax
import jax.numpy as jnp
from jax import lax
from jax.experimental import pallas as pl
from jax.experimental.pallas import tpu as pltpu
from jax.sharding import PartitionSpec as P

HD = 128
SEQS = 4
GROUP = 8
BETA = 2.0
LOSS_SCALE = 1024.0
NEG_FILL = -1e30
LOG2E = 1.4426950408889634
SCALE = HD**-0.5
WINDOW = 5
CTX = 8
HEADS = (4, 4)
F32 = jnp.float32
BF16 = jnp.bfloat16
NT = (((1,), (1,)), ((), ()))
TN = (((0,), (0,)), ((), ()))
VMEM = pl.BlockSpec(memory_space=pltpu.VMEM)
SMEM = pl.BlockSpec(memory_space=pltpu.SMEM)

SIBLING = [(i, i ^ 1) for i in range(CTX)]


def shift(by):
    return [(i, i + by) for i in range(CTX) if 0 <= i + by < CTX]


def cut(at, width):
    return slice(at * width, (at + 1) * width)


def pick_row(array, row):
    rows = lax.broadcasted_iota(jnp.int32, array.shape, 0)
    return jnp.sum(jnp.where(rows == row, array, 0), axis=0, keepdims=True)


def window_bias(rank, place, seg_ref, tok):
    pack = pick_row(seg_ref[...], rank)
    mine = pick_row(seg_ref[:, pl.ds(pl.multiple_of(place * tok, tok), tok)], rank)
    start = jnp.zeros((1, tok), jnp.int32)
    for slot in range(SEQS - 1):
        count = jnp.sum((pack == slot).astype(F32)).astype(jnp.int32)
        start = start + jnp.where(mine > slot, count, 0)
    last = place * tok + lax.broadcasted_iota(jnp.int32, (1, tok), 1)
    core = lax.rem(place, 2)
    at = lax.broadcasted_iota(jnp.int32, (tok, tok), 0)
    parts = []
    for block in (place, place - 2, place - 4, place - 1 - 2 * core, place - 3 + 2 * core):
        pos = at + block * tok
        parts.append(jnp.where((pos >= start) & (pos <= last), 0.0, NEG_FILL))
    return jnp.concatenate(parts, axis=0), mine


def attend(first, heads, final, where_ref, seg_ref, term_in, q_ref, u_ref, *refs):
    tok = q_ref.shape[0]
    width = heads * HD
    blocks = refs[:WINDOW]
    dq_ref, term_ref, near_ref, far_ref, pair_ref, own_ref = refs[WINDOW:]
    bias, mine = window_bias(where_ref[0], where_ref[1], seg_ref, tok)
    bias = jnp.concatenate([bias] * GROUP, axis=1)
    term = term_in[...]
    for head in range(heads):
        keys = jnp.concatenate([ref[:, cut(head, HD)] for ref in blocks], axis=0)
        values = jnp.concatenate([ref[:, cut(heads + head, HD)] for ref in blocks], axis=0)
        base = (first + head) * GROUP
        q = jnp.concatenate([q_ref[:, cut(base + g, HD)] for g in range(GROUP)], axis=0)
        u = jnp.concatenate([u_ref[:, cut(base + g, HD)] for g in range(GROUP)], axis=0)
        scores = lax.dot_general(keys, q, NT, preferred_element_type=F32)
        scores = scores * (SCALE * LOG2E) + bias
        expo = jnp.exp2(scores - jnp.max(scores, axis=0, keepdims=True))
        probs = expo * (1.0 / jnp.sum(expo, axis=0, keepdims=True))
        dprob = lax.dot_general(values, u, NT, preferred_element_type=F32)
        delta = jnp.sum(probs * dprob, axis=0, keepdims=True)
        dscore = (probs * (dprob - delta)).astype(BF16)
        dv = jnp.dot(probs.astype(BF16), u, preferred_element_type=F32)
        dk = jnp.dot(dscore, q, preferred_element_type=F32) * SCALE
        dq = lax.dot_general(dscore, keys, TN, preferred_element_type=F32) * SCALE
        for g in range(GROUP):
            term = term + delta[:, cut(g, tok)]
            dq_ref[:, cut(head * GROUP + g, HD)] = dq[cut(g, tok)].astype(BF16)
        for side, part in ((head, dk), (heads + head, dv)):
            cols = cut(side, HD)
            own_ref[:, cols] = part[:tok]
            near_ref[:, cols] = part[cut(1, tok)].astype(BF16)
            far_ref[:, cols] = part[cut(2, tok)].astype(BF16)
            pair_ref[:, cols] = part[3 * tok :].astype(BF16)
    if final:
        lane = lax.broadcasted_iota(jnp.int32, (1, HD), 1)
        row = jnp.zeros((1, HD), F32)
        for slot in range(SEQS):
            total = jnp.sum(jnp.where(mine == slot, term, 0.0), axis=1, keepdims=True)
            row = row + jnp.where(lane == where_ref[0] * SEQS + slot, total, 0.0)
        term_ref[...] = jnp.broadcast_to(row, term_ref.shape)
    else:
        term_ref[...] = term


def attend_part(part, devices, where, segments, term, queries, upstream, blocks):
    tok = queries.shape[0]
    heads = HEADS[part]
    final = part == len(HEADS) - 1
    width = 2 * heads * HD
    shapes = [
        ((tok, heads * GROUP * HD), BF16),
        ((devices, HD) if final else (1, tok), F32),
        ((tok, width), BF16),
        ((tok, width), BF16),
        ((2 * tok, width), BF16),
        ((tok, width), F32),
    ]
    return pl.pallas_call(
        functools.partial(attend, sum(HEADS[:part]), heads, final),
        in_specs=[SMEM] + [VMEM] * (4 + WINDOW),
        out_specs=[VMEM] * len(shapes),
        out_shape=[jax.ShapeDtypeStruct(shape, dtype) for shape, dtype in shapes],
        compiler_params=pltpu.CompilerParams(vmem_limit_bytes=28 * 2**20),
        cost_estimate=pl.CostEstimate(
            flops=20 * heads * GROUP * tok * WINDOW * tok * HD,
            bytes_accessed=8 * tok * heads * GROUP * HD,
            transcendentals=heads * GROUP * tok * WINDOW * tok,
        ),
    )(where, segments, term, queries, upstream, *blocks)


def merge(where_ref, near_ref, far_ref, pair_ref, own_ref, near_out, far_out, own_out):
    tok = near_ref.shape[0]
    core = lax.rem(where_ref[1], 2).astype(F32)
    near_out[...] = (near_ref[...].astype(F32) + pair_ref[:tok].astype(F32)).astype(BF16)
    fifth = pair_ref[tok:].astype(F32)
    far_out[...] = (far_ref[...].astype(F32) + core * fifth).astype(BF16)
    own_out[...] = own_ref[...] + (1.0 - core) * fifth


def merge_part(where, near, far, pair, own):
    return pl.pallas_call(
        merge,
        in_specs=[SMEM] + [VMEM] * 4,
        out_specs=[VMEM] * 3,
        out_shape=[jax.ShapeDtypeStruct(a.shape, a.dtype) for a in (near, far, own)],
    )(where, near, far, pair, own)


def weigh(where_ref, every_ref, seg_ref, partner_ref, chosen_ref, score_ref, loss_ref):
    rank, place = where_ref[0], where_ref[1]
    packs = seg_ref.shape[0]
    lane = lax.broadcasted_iota(jnp.int32, (1, HD), 1)
    row = lax.broadcasted_iota(jnp.int32, (HD, HD), 0)
    col = lax.broadcasted_iota(jnp.int32, (HD, HD), 1)
    eye = row == col
    seg = seg_ref[...]
    counts = jnp.zeros((packs, HD), F32)
    for slot in range(SEQS):
        count = jnp.sum((seg == slot).astype(F32), axis=1, keepdims=True)
        counts = counts + jnp.where(lax.rem(lane, SEQS) == slot, count, 0.0)
    pack_of = lax.broadcasted_iota(jnp.int32, (packs, HD), 0) * SEQS
    held = (lane >= pack_of) & (lane < pack_of + SEQS)
    lengths = jnp.sum(jnp.where(held, counts, 0.0), axis=0, keepdims=True)
    totals = jnp.sum(every_ref[...], axis=0, keepdims=True)
    adjusted = totals / lengths - score_ref[...]
    adjusted_col = jnp.sum(jnp.where(eye, adjusted, 0.0), axis=1, keepdims=True)
    mate = jnp.sum(jnp.where(row == partner_ref[...], adjusted_col, 0.0), axis=0, keepdims=True)
    chosen = chosen_ref[...].astype(F32)
    sign = 2.0 * chosen - 1.0
    margin = BETA * sign * (adjusted - mate)
    softplus = jnp.maximum(-margin, 0.0) + jnp.log1p(jnp.exp(-jnp.abs(margin)))
    loss_ref[0, 0] = jnp.sum(chosen * softplus)
    weight = -sign * BETA * LOSS_SCALE / (1.0 + jnp.exp(margin)) / lengths
    mine = pick_row(seg_ref[:, pl.ds(pl.multiple_of(place * HD, HD), HD)], rank)
    mine_col = jnp.sum(jnp.where(eye, mine.astype(F32), 0.0), axis=1, keepdims=True)
    hit = col == mine_col.astype(jnp.int32) + rank * SEQS
    return jnp.sum(jnp.where(hit, weight, 0.0), axis=1, keepdims=True)


def finish(where_ref, every_ref, seg_ref, partner_ref, chosen_ref, score_ref, *refs):
    parts = len(HEADS)
    dq_refs, sides = refs[:parts], refs[parts : 4 * parts]
    out_q, out_k, out_v, loss_ref, weight_ref = refs[4 * parts :]
    step = pl.program_id(0)

    @pl.when(step == 0)
    def _():
        weight = weigh(
            where_ref, every_ref, seg_ref, partner_ref, chosen_ref, score_ref, loss_ref
        )
        weight_ref[...] = jnp.broadcast_to(weight, weight_ref.shape)
        first = 0
        for part, heads in enumerate(HEADS):
            own, near, far = sides[3 * part : 3 * part + 3]
            width = heads * HD
            for out, cols in ((out_k, slice(0, width)), (out_v, slice(width, 2 * width))):
                side = own[:, cols] + near[:, cols].astype(F32) + far[:, cols].astype(F32)
                out[:, first : first + width] = (side * weight).astype(BF16)
            first += width

    weight = weight_ref[...]
    first = 0
    for part, heads in enumerate(HEADS):

        @pl.when((step >= first) & (step < first + heads))
        def _(part=part):
            for g in range(GROUP):
                cols = cut(g, HD)
                out_q[:, cols] = (dq_refs[part][:, cols].astype(F32) * weight).astype(BF16)

        first += heads


def finish_all(where, every, segments, partner, chosen, score, grad_q, sides):
    tok = grad_q[0].shape[0]
    steps = sum(HEADS)
    wide = GROUP * HD

    def whole(array):
        return pl.BlockSpec(array.shape, lambda i: (0, 0))

    q_specs = []
    first = 0
    for heads in HEADS:
        q_specs.append(
            pl.BlockSpec(
                (tok, wide),
                lambda i, first=first, heads=heads: (0, jnp.clip(i - first, 0, heads - 1)),
            )
        )
        first += heads
    small = (every, segments, partner, chosen, score)
    flat = [array for side in sides for array in side]
    kv_shape = jax.ShapeDtypeStruct((tok, steps * HD), BF16)
    kv_spec = pl.BlockSpec(kv_shape.shape, lambda i: (0, 0))
    return pl.pallas_call(
        finish,
        grid=(steps,),
        in_specs=[SMEM] + [whole(a) for a in small] + q_specs + [whole(a) for a in flat],
        out_specs=[pl.BlockSpec((tok, wide), lambda i: (0, i)), kv_spec, kv_spec, SMEM],
        out_shape=[
            jax.ShapeDtypeStruct((tok, steps * wide), BF16),
            kv_shape,
            kv_shape,
            jax.ShapeDtypeStruct((1, 1), F32),
        ],
        scratch_shapes=[pltpu.VMEM((tok, HD), F32)],
        compiler_params=pltpu.CompilerParams(vmem_limit_bytes=28 * 2**20),
    )(where, *small, *grad_q, *flat)


def after(value, *others):
    return lax.optimization_barrier((value, *others))[0]


def per_device(queries, keys, values, upstream, token_logp, segments, partner, chosen, ref_score):
    place = lax.axis_index("ctx")
    where = jnp.stack([lax.axis_index("dp"), place]).astype(jnp.int32)
    core = place % 2
    devices = lax.axis_size("dp") * CTX
    parts = range(len(HEADS))
    edges = [sum(HEADS[:part]) * HD for part in range(len(HEADS) + 1)]

    own, near, far = [], [], []
    for part in parts:
        cols = slice(edges[part], edges[part + 1])
        block = jnp.concatenate([keys[0][:, cols], values[0][:, cols]], axis=1)
        own.append(block)
        send_near = send_far = block
        if part:
            send_near, send_far = after(block, near[-1]), after(block, far[-1])
        near.append(lax.ppermute(send_near, "ctx", shift(2)))
        far.append(lax.ppermute(send_far, "ctx", shift(4)))

    term = token_logp
    grad_q, returns = [], []
    for part in parts:
        here, there = near[part], far[part]
        if part:
            here, there, _ = lax.optimization_barrier((here, there, term))
        near_pair = lax.ppermute(here, "ctx", SIBLING)
        fifth = lax.ppermute(jnp.where(core == 0, own[part], there), "ctx", SIBLING)
        blocks = (own[part], here, there, near_pair, fifth)
        dq, term, to_near, to_far, to_pair, mine = attend_part(
            part, devices, where, segments, term, queries[0], upstream[0], blocks
        )
        grad_q.append(dq)
        pair = lax.ppermute(to_pair, "ctx", SIBLING)
        near_sum, far_sum, mine = merge_part(where, to_near, to_far, pair, mine)
        near_back = lax.ppermute(near_sum, "ctx", shift(-2))
        far_back = lax.ppermute(far_sum, "ctx", shift(-4))
        returns.append((mine, near_back, far_back))

    every = lax.all_to_all(term, ("dp", "ctx"), split_axis=0, concat_axis=0, tiled=True)
    out_q, out_k, out_v, loss = finish_all(
        where,
        every,
        segments,
        partner[None],
        chosen[None],
        ref_score[None],
        grad_q,
        returns,
    )
    return out_q[None], out_k[None], out_v[None], loss.reshape(())


def solution(mesh):
    return jax.shard_map(
        per_device,
        mesh=mesh,
        in_specs=(
            P("dp", "ctx", None),
            P("dp", "ctx", None),
            P("dp", "ctx", None),
            P("dp", "ctx", None),
            P("dp", "ctx"),
            P(),
            P(),
            P(),
            P(),
        ),
        out_specs=(P("dp", "ctx", None), P("dp", "ctx", None), P("dp", "ctx", None), P()),
        check_vma=False,
    )
```

```python
import functools

import jax
import jax.numpy as jnp
from jax import lax
from jax.experimental import pallas as pl
from jax.experimental.pallas import tpu as pltpu
from jax.sharding import PartitionSpec as P

HD = 128
SEQS = 4
GROUP = 8
BETA = 2.0
LOSS_SCALE = 1024.0
NEG_FILL = -1e30
LOG2E = 1.4426950408889634
SCALE = HD**-0.5
WINDOW = 5
CTX = 8
VMEM_BYTES = 24 * 2**20
CHUNK = 2
HEADS = (4, 4)
PER_STEP = 2
F32 = jnp.float32
BF16 = jnp.bfloat16
NT = (((1,), (1,)), ((), ()))
TN = (((0,), (0,)), ((), ()))
VMEM = pl.BlockSpec(memory_space=pltpu.VMEM)
LIGHT = pl.CostEstimate(flops=1000, bytes_accessed=1000, transcendentals=0)
SMEM = pl.BlockSpec(memory_space=pltpu.SMEM)

SIBLING = [(i, i ^ 1) for i in range(CTX)]


def shift(by):
    return [(i, i + by) for i in range(CTX) if 0 <= i + by < CTX]


def cut(at, width):
    return slice(at * width, (at + 1) * width)


def pick_row(array, row):
    rows = lax.broadcasted_iota(jnp.int32, array.shape, 0)
    return jnp.sum(jnp.where(rows == row, array, 0), axis=0, keepdims=True)


def window_bias(rank, place, seg_ref, tok):
    pack = pick_row(seg_ref[...], rank)
    mine = pick_row(seg_ref[:, pl.ds(pl.multiple_of(place * tok, tok), tok)], rank)
    start = jnp.zeros((1, tok), jnp.int32)
    for slot in range(SEQS - 1):
        count = jnp.sum((pack == slot).astype(F32)).astype(jnp.int32)
        start = start + jnp.where(mine > slot, count, 0)
    last = place * tok + lax.broadcasted_iota(jnp.int32, (1, tok), 1)
    core = lax.rem(place, 2)
    at = lax.broadcasted_iota(jnp.int32, (tok, tok), 0)
    parts = []
    for block in (place, place - 2, place - 4, place - 1 - 2 * core, place - 3 + 2 * core):
        pos = at + block * tok
        parts.append(jnp.where((pos >= start) & (pos <= last), 0.0, NEG_FILL))
    return jnp.concatenate(parts, axis=0), mine


def lengths_row(seg):
    packs = seg.shape[0]
    lane = lax.broadcasted_iota(jnp.int32, (1, HD), 1)
    counts = jnp.zeros((packs, HD), F32)
    for slot in range(SEQS):
        count = jnp.sum((seg == slot).astype(F32), axis=1, keepdims=True)
        counts = counts + jnp.where(lax.rem(lane, SEQS) == slot, count, 0.0)
    pack_of = lax.broadcasted_iota(jnp.int32, (packs, HD), 0) * SEQS
    held = (lane >= pack_of) & (lane < pack_of + SEQS)
    return jnp.sum(jnp.where(held, counts, 0.0), axis=0, keepdims=True)


def stage(where_ref, seg_ref, q_ref, u_ref, bias_ref, hit_ref, length_ref, *stacks):
    tok = q_ref.shape[0]
    rank = where_ref[0]
    bias_ref[...], mine = window_bias(rank, where_ref[1], seg_ref, tok)
    length_ref[...] = lengths_row(seg_ref[...])
    row = lax.broadcasted_iota(jnp.int32, (tok, HD), 0)
    col = lax.broadcasted_iota(jnp.int32, (tok, HD), 1)
    mine = jnp.sum(jnp.where(row == col, mine.astype(F32), 0.0), axis=1, keepdims=True)
    hit_ref[...] = (col == mine.astype(jnp.int32) + rank * SEQS).astype(F32)
    parts = len(HEADS)
    for source, outs in ((q_ref, stacks[:parts]), (u_ref, stacks[parts:])):
        first = 0
        for out, heads in zip(outs, HEADS):
            for g in range(heads * GROUP):
                out[cut(g, tok), :] = source[:, cut(first + g, HD)]
            first += heads * GROUP


def window(blocks, head):
    return jnp.concatenate([ref[:, cut(head, HD)] for ref in blocks], axis=0)


def forward_chunk(keys, values, q, u, bias):
    scores = lax.dot_general(keys, q, NT, preferred_element_type=F32)
    scores = scores * (SCALE * LOG2E) + bias
    expo = jnp.exp2(scores - jnp.max(scores, axis=0, keepdims=True))
    probs = expo * (1.0 / jnp.sum(expo, axis=0, keepdims=True))
    dprob = lax.dot_general(values, u, NT, preferred_element_type=F32)
    delta = jnp.sum(probs * dprob, axis=0, keepdims=True)
    dscore = (probs * (dprob - delta)).astype(BF16)
    return probs.astype(BF16), dscore, delta


def forward_head(keys, values, q, u, bias):
    chunks = []
    for at in range(GROUP // CHUNK):
        rows = cut(at, q.shape[0] // (GROUP // CHUNK))
        chunks.append(forward_chunk(keys, values, q[rows], u[rows], bias))
    return (jnp.concatenate(side, axis=1) for side in zip(*chunks))


def backward_head(head, keys, q, u, probs, dscore, outs):
    dq_ref, near_ref, far_ref, pair_ref, own_ref = outs
    tok = near_ref.shape[1]
    dv = jnp.dot(probs, u, preferred_element_type=F32)
    dk = jnp.dot(dscore, q, preferred_element_type=F32) * SCALE
    dq = lax.dot_general(dscore, keys, TN, preferred_element_type=F32) * SCALE
    for g in range(GROUP):
        dq_ref[:, cut(head * GROUP + g, HD)] = dq[cut(g, tok)].astype(BF16)
    cols = cut(head, HD)
    for side, part in enumerate((dk, dv)):
        own_ref[side, :, cols] = part[:tok]
        near_ref[side, :, cols] = part[cut(1, tok)].astype(BF16)
        far_ref[side, :, cols] = part[cut(2, tok)].astype(BF16)
        pair_ref[0, side, :, cols] = part[cut(3, tok)].astype(BF16)
        pair_ref[1, side, :, cols] = part[cut(4, tok)].astype(BF16)


def backward_shapes(tok, heads):
    width = heads * HD
    return [
        ((tok, heads * GROUP * HD), BF16),
        ((2, tok, width), BF16),
        ((2, tok, width), BF16),
        ((2, 2, tok, width), BF16),
        ((2, tok, width), F32),
    ]


def local_call(kernel, args, shapes, cost, scalars=0):
    return pl.pallas_call(
        kernel,
        in_specs=[SMEM] * scalars + [VMEM] * (len(args) - scalars),
        out_specs=[VMEM] * len(shapes),
        out_shape=[jax.ShapeDtypeStruct(shape, dtype) for shape, dtype in shapes],
        compiler_params=pltpu.CompilerParams(vmem_limit_bytes=VMEM_BYTES),
        cost_estimate=cost,
    )(*args)


def attend(heads, final, where_ref, seg_ref, term_in, bias_ref, q_ref, u_ref, *refs):
    blocks, term_ref, outs = refs[:-6], refs[-6], refs[-5:]
    tok = bias_ref.shape[1]
    bias = jnp.concatenate([bias_ref[...]] * CHUNK, axis=1)
    term = term_in[...]
    for head in range(heads):
        keys, values = window(blocks, head), window(blocks, heads + head)
        rows = cut(head, GROUP * tok)
        q, u = q_ref[rows, :], u_ref[rows, :]
        probs, dscore, delta = forward_head(keys, values, q, u, bias)
        for g in range(GROUP):
            term = term + delta[:, cut(g, tok)]
        backward_head(head, keys, q, u, probs, dscore, outs)
    if final:
        rank, place = where_ref[0], where_ref[1]
        mine = pick_row(seg_ref[:, pl.ds(pl.multiple_of(place * tok, tok), tok)], rank)
        lane = lax.broadcasted_iota(jnp.int32, (1, HD), 1)
        row = jnp.zeros((1, HD), F32)
        for slot in range(SEQS):
            total = jnp.sum(jnp.where(mine == slot, term, 0.0), axis=1, keepdims=True)
            row = row + jnp.where(lane == rank * SEQS + slot, total, 0.0)
        term_ref[...] = jnp.broadcast_to(row, term_ref.shape)
    else:
        term_ref[...] = term


def merge(where_ref, *refs):
    near_out, far_out = refs[-2:]
    core = lax.rem(where_ref[1], 2).astype(F32)
    first = 0
    for part, heads in enumerate(HEADS):
        near, far, pair = refs[3 * part : 3 * part + 3]
        cols = slice(first, first + heads * HD)
        near_out[:, :, cols] = (near[...].astype(F32) + pair[0].astype(F32)).astype(BF16)
        far_out[:, :, cols] = (far[...].astype(F32) + core * pair[1].astype(F32)).astype(BF16)
        first += heads * HD


def weigh(every_ref, length_ref, hit_ref, partner_ref, chosen_ref, score_ref, loss_ref):
    row = lax.broadcasted_iota(jnp.int32, (HD, HD), 0)
    col = lax.broadcasted_iota(jnp.int32, (HD, HD), 1)
    lengths = length_ref[...]
    totals = jnp.sum(every_ref[...], axis=0, keepdims=True)
    adjusted = totals / lengths - score_ref[...]
    adjusted_col = jnp.sum(jnp.where(row == col, adjusted, 0.0), axis=1, keepdims=True)
    mate = jnp.sum(jnp.where(row == partner_ref[...], adjusted_col, 0.0), axis=0, keepdims=True)
    chosen = chosen_ref[...].astype(F32)
    sign = 2.0 * chosen - 1.0
    margin = BETA * sign * (adjusted - mate)
    softplus = jnp.maximum(-margin, 0.0) + jnp.log1p(jnp.exp(-jnp.abs(margin)))
    loss_ref[0, 0] = jnp.sum(chosen * softplus)
    weight = -sign * BETA * LOSS_SCALE / (1.0 + jnp.exp(margin)) / lengths
    return jnp.sum(hit_ref[...] * weight, axis=1, keepdims=True)


def finish(where_ref, *refs):
    small, refs = refs[:6], refs[6:]
    parts = len(HEADS)
    dq_refs, own_refs, pair_refs = (refs[i * parts : (i + 1) * parts] for i in range(3))
    near, far, out_q, out_k, out_v, loss_ref, weight_ref = refs[3 * parts :]
    step = pl.program_id(0)

    @pl.when(step == 0)
    def _():
        weight = weigh(*small, loss_ref)
        weight_ref[...] = jnp.broadcast_to(weight, weight_ref.shape)

    weight = weight_ref[...]
    even = 1.0 - lax.rem(where_ref[1], 2).astype(F32)
    origin = [(part, head) for part, heads in enumerate(HEADS) for head in range(heads)]
    for at in range(len(origin) // PER_STEP):

        @pl.when(step == at)
        def _(at=at):
            for here in range(PER_STEP):
                part, local = origin[at * PER_STEP + here]
                cols, back = cut(local, HD), cut(at * PER_STEP + here, HD)
                for out, base in ((out_k, 0), (out_v, 1)):
                    side = own_refs[part][base, :, cols]
                    side = side + even * pair_refs[part][1, base, :, cols].astype(F32)
                    side = side + near[base, :, back].astype(F32)
                    side = side + far[base, :, back].astype(F32)
                    out[:, cut(here, HD)] = (side * weight).astype(BF16)
                for g in range(GROUP):
                    dq = dq_refs[part][:, cut(local * GROUP + g, HD)].astype(F32)
                    out_q[:, cut(here * GROUP + g, HD)] = (dq * weight).astype(BF16)


def finish_all(where, small, grad_q, mines, pairs, backs):
    tok = grad_q[0].shape[0]
    steps = sum(HEADS) // PER_STEP
    arrays = [*small, *grad_q, *mines, *pairs, *backs]
    widths = [PER_STEP * GROUP * HD, PER_STEP * HD, PER_STEP * HD]
    return pl.pallas_call(
        finish,
        grid=(steps,),
        in_specs=[SMEM] + [VMEM] * len(arrays),
        out_specs=[pl.BlockSpec((tok, width), lambda i: (0, i)) for width in widths] + [SMEM],
        out_shape=[jax.ShapeDtypeStruct((tok, steps * width), BF16) for width in widths]
        + [jax.ShapeDtypeStruct((1, 1), F32)],
        scratch_shapes=[pltpu.VMEM((tok, HD), F32)],
        compiler_params=pltpu.CompilerParams(vmem_limit_bytes=VMEM_BYTES),
    )(where, *arrays)


def gather_window(own, near, far, core, halves):
    pairs = [near, jnp.where(core == 0, own, far)]
    if halves:
        half = near.shape[0] // 2
        pairs = [array[rows] for array in pairs for rows in (slice(0, half), slice(half, None))]
    pairs = [lax.ppermute(array, "ctx", SIBLING) for array in pairs]
    return (own, near, far, *pairs)


def tie(value, *others):
    return lax.optimization_barrier((value, *others))[0]


def per_device(queries, keys, values, upstream, token_logp, segments, partner, chosen, ref_score):
    place = lax.axis_index("ctx")
    where = jnp.stack([lax.axis_index("dp"), place]).astype(jnp.int32)
    core = place % 2
    tok = queries.shape[1]
    devices = lax.axis_size("dp") * CTX
    own, near, far = [], [], []
    first = 0
    for heads in HEADS:
        cols = slice(first * HD, (first + heads) * HD)
        block = jnp.concatenate([keys[0][:, cols], values[0][:, cols]], axis=1)
        own.append(block)
        near.append(lax.ppermute(block, "ctx", shift(2)))
        far.append(lax.ppermute(block, "ctx", shift(4)))
        first += heads
    parts = len(HEADS)
    bias, hit, lengths, *stacks = local_call(
        stage,
        (where, segments, queries[0], upstream[0]),
        [((WINDOW * tok, tok), F32), ((tok, HD), F32), ((1, HD), F32)]
        + [((heads * GROUP * tok, HD), BF16) for heads in HEADS] * 2,
        None,
        1,
    )

    term = token_logp
    grad_q, mines, pairs, outward = [], [], [], []
    for part, heads in enumerate(HEADS):
        final = part == len(HEADS) - 1
        ready = term if part else bias
        here, there, _ = lax.optimization_barrier((near[part], far[part], ready))
        blocks = gather_window(own[part], here, there, core, part == 0)
        term, dq, to_near, to_far, to_pair, mine = local_call(
            functools.partial(attend, heads, final),
            (where, segments, term, bias, stacks[part], stacks[parts + part], *blocks),
            [((devices, HD) if final else (1, tok), F32)] + backward_shapes(tok, heads),
            LIGHT,
            1,
        )
        grad_q.append(dq)
        mines.append(mine)
        pairs.append(lax.ppermute(to_pair, "ctx", SIBLING))
        outward += [to_near, to_far, pairs[-1]]
    shape = ((2, tok, sum(HEADS) * HD), BF16)
    near_sum, far_sum = local_call(merge, (where, *outward), [shape] * 2, LIGHT, 1)
    backs = (
        lax.ppermute(near_sum, "ctx", shift(-2)),
        lax.ppermute(far_sum, "ctx", shift(-4)),
    )

    term = tie(term, near_sum, far_sum)
    every = lax.all_to_all(term, ("dp", "ctx"), split_axis=0, concat_axis=0, tiled=True)
    small = (every, lengths, hit, partner[None], chosen[None], ref_score[None])
    out_q, out_k, out_v, loss = finish_all(where, small, grad_q, mines, pairs, backs)
    return out_q[None], out_k[None], out_v[None], loss.reshape(())


def solution(mesh):
    return jax.shard_map(
        per_device,
        mesh=mesh,
        in_specs=(
            P("dp", "ctx", None),
            P("dp", "ctx", None),
            P("dp", "ctx", None),
            P("dp", "ctx", None),
            P("dp", "ctx"),
            P(),
            P(),
            P(),
            P(),
        ),
        out_specs=(P("dp", "ctx", None), P("dp", "ctx", None), P("dp", "ctx", None), P()),
        check_vma=False,
    )
```

```python
import functools

import jax
import jax.numpy as jnp
from jax import lax
from jax.experimental import pallas as pl
from jax.experimental.pallas import tpu as pltpu
from jax.sharding import PartitionSpec as P

HD = 128
SEQS = 4
GROUP = 8
BETA = 2.0
LOSS_SCALE = 1024.0
NEG_FILL = -1e30
LOG2E = 1.4426950408889634
SCALE = HD**-0.5
WINDOW = 5
CTX = 8
VMEM_BYTES = 24 * 2**20
CHUNK = 2
HEADS = (4, 4)
PER_STEP = 4
F32 = jnp.float32
BF16 = jnp.bfloat16
NT = (((1,), (1,)), ((), ()))
TN = (((0,), (0,)), ((), ()))
VMEM = pl.BlockSpec(memory_space=pltpu.VMEM)
LIGHT = pl.CostEstimate(flops=1000, bytes_accessed=1000, transcendentals=0)
SMEM = pl.BlockSpec(memory_space=pltpu.SMEM)

SIBLING = [(i, i ^ 1) for i in range(CTX)]


def shift(by):
    return [(i, i + by) for i in range(CTX) if 0 <= i + by < CTX]


def cut(at, width):
    return slice(at * width, (at + 1) * width)


def pick_row(array, row):
    rows = lax.broadcasted_iota(jnp.int32, array.shape, 0)
    return jnp.sum(jnp.where(rows == row, array, 0), axis=0, keepdims=True)


def window_bias(rank, place, seg_ref, tok):
    pack = pick_row(seg_ref[...], rank)
    mine = pick_row(seg_ref[:, pl.ds(pl.multiple_of(place * tok, tok), tok)], rank)
    start = jnp.zeros((1, tok), jnp.int32)
    for slot in range(SEQS - 1):
        count = jnp.sum((pack == slot).astype(F32)).astype(jnp.int32)
        start = start + jnp.where(mine > slot, count, 0)
    last = place * tok + lax.broadcasted_iota(jnp.int32, (1, tok), 1)
    core = lax.rem(place, 2)
    at = lax.broadcasted_iota(jnp.int32, (tok, tok), 0)
    parts = []
    for block in (place, place - 2, place - 4, place - 1 - 2 * core, place - 3 + 2 * core):
        pos = at + block * tok
        parts.append(jnp.where((pos >= start) & (pos <= last), 0.0, NEG_FILL))
    return jnp.concatenate(parts, axis=0), mine


def lengths_row(seg):
    packs = seg.shape[0]
    lane = lax.broadcasted_iota(jnp.int32, (1, HD), 1)
    counts = jnp.zeros((packs, HD), F32)
    for slot in range(SEQS):
        count = jnp.sum((seg == slot).astype(F32), axis=1, keepdims=True)
        counts = counts + jnp.where(lax.rem(lane, SEQS) == slot, count, 0.0)
    pack_of = lax.broadcasted_iota(jnp.int32, (packs, HD), 0) * SEQS
    held = (lane >= pack_of) & (lane < pack_of + SEQS)
    return jnp.sum(jnp.where(held, counts, 0.0), axis=0, keepdims=True)


def stage(where_ref, seg_ref, q_ref, u_ref, bias_ref, hit_ref, length_ref, *stacks):
    tok = q_ref.shape[0]
    rank = where_ref[0]
    bias_ref[...], mine = window_bias(rank, where_ref[1], seg_ref, tok)
    length_ref[...] = lengths_row(seg_ref[...])
    row = lax.broadcasted_iota(jnp.int32, (tok, HD), 0)
    col = lax.broadcasted_iota(jnp.int32, (tok, HD), 1)
    mine = jnp.sum(jnp.where(row == col, mine.astype(F32), 0.0), axis=1, keepdims=True)
    hit_ref[...] = (col == mine.astype(jnp.int32) + rank * SEQS).astype(F32)
    parts = len(HEADS)
    for source, outs in ((q_ref, stacks[:parts]), (u_ref, stacks[parts:])):
        first = 0
        for out, heads in zip(outs, HEADS):
            for g in range(heads * GROUP):
                out[cut(g, tok), :] = source[:, cut(first + g, HD)]
            first += heads * GROUP


def window(blocks, head):
    return jnp.concatenate([ref[:, cut(head, HD)] for ref in blocks], axis=0)


def forward_chunk(keys, values, q, u, bias):
    scores = lax.dot_general(keys, q, NT, preferred_element_type=F32)
    scores = scores * (SCALE * LOG2E) + bias
    expo = jnp.exp2(scores - jnp.max(scores, axis=0, keepdims=True))
    share = 1.0 / jnp.sum(expo, axis=0, keepdims=True)
    probs = expo.astype(BF16) * share.astype(BF16)
    dprob = lax.dot_general(values, u, NT, preferred_element_type=F32)
    delta = jnp.sum(expo * dprob, axis=0, keepdims=True) * share
    return probs, probs * (dprob - delta).astype(BF16), delta


def forward_head(keys, values, q, u, bias):
    chunks = []
    for at in range(GROUP // CHUNK):
        rows = cut(at, q.shape[0] // (GROUP // CHUNK))
        chunks.append(forward_chunk(keys, values, q[rows], u[rows], bias))
    return (jnp.concatenate(side, axis=1) for side in zip(*chunks))


def backward_head(head, keys, q, u, probs, dscore, outs):
    dq_ref, near_ref, far_ref, pair_ref, own_ref = outs
    tok = near_ref.shape[1]
    dv = jnp.dot(probs, u, preferred_element_type=F32)
    dk = jnp.dot(dscore, q, preferred_element_type=F32) * SCALE
    dq = lax.dot_general(dscore, keys, TN, preferred_element_type=F32) * SCALE
    for g in range(GROUP):
        dq_ref[:, cut(head * GROUP + g, HD)] = dq[cut(g, tok)].astype(BF16)
    cols = cut(head, HD)
    for side, part in enumerate((dk, dv)):
        own_ref[side, :, cols] = part[:tok]
        near_ref[side, :, cols] = part[cut(1, tok)].astype(BF16)
        far_ref[side, :, cols] = part[cut(2, tok)].astype(BF16)
        pair_ref[0, side, :, cols] = part[cut(3, tok)].astype(BF16)
        pair_ref[1, side, :, cols] = part[cut(4, tok)].astype(BF16)


def backward_shapes(tok, heads):
    width = heads * HD
    return [
        ((tok, heads * GROUP * HD), BF16),
        ((2, tok, width), BF16),
        ((2, tok, width), BF16),
        ((2, 2, tok, width), BF16),
        ((2, tok, width), F32),
    ]


def local_call(kernel, args, shapes, cost, scalars=0):
    return pl.pallas_call(
        kernel,
        in_specs=[SMEM] * scalars + [VMEM] * (len(args) - scalars),
        out_specs=[VMEM] * len(shapes),
        out_shape=[jax.ShapeDtypeStruct(shape, dtype) for shape, dtype in shapes],
        compiler_params=pltpu.CompilerParams(vmem_limit_bytes=VMEM_BYTES),
        cost_estimate=cost,
    )(*args)


def attend(heads, final, where_ref, seg_ref, term_in, bias_ref, q_ref, u_ref, *refs):
    blocks, term_ref, outs = refs[:-6], refs[-6], refs[-5:]
    tok = bias_ref.shape[1]
    bias = jnp.concatenate([bias_ref[...]] * CHUNK, axis=1)
    term = term_in[...]
    for head in range(heads):
        keys, values = window(blocks, head), window(blocks, heads + head)
        rows = cut(head, GROUP * tok)
        q, u = q_ref[rows, :], u_ref[rows, :]
        probs, dscore, delta = forward_head(keys, values, q, u, bias)
        for g in range(GROUP):
            term = term + delta[:, cut(g, tok)]
        backward_head(head, keys, q, u, probs, dscore, outs)
    if final:
        rank, place = where_ref[0], where_ref[1]
        mine = pick_row(seg_ref[:, pl.ds(pl.multiple_of(place * tok, tok), tok)], rank)
        lane = lax.broadcasted_iota(jnp.int32, (1, HD), 1)
        row = jnp.zeros((1, HD), F32)
        for slot in range(SEQS):
            total = jnp.sum(jnp.where(mine == slot, term, 0.0), axis=1, keepdims=True)
            row = row + jnp.where(lane == rank * SEQS + slot, total, 0.0)
        term_ref[...] = jnp.broadcast_to(row, term_ref.shape)
    else:
        term_ref[...] = term


def merge(where_ref, *refs):
    near_out, far_out = refs[-2:]
    core = lax.rem(where_ref[1], 2).astype(F32)
    first = 0
    for part, heads in enumerate(HEADS):
        near, far, pair = refs[3 * part : 3 * part + 3]
        cols = slice(first, first + heads * HD)
        near_out[:, :, cols] = (near[...].astype(F32) + pair[0].astype(F32)).astype(BF16)
        far_out[:, :, cols] = (far[...].astype(F32) + core * pair[1].astype(F32)).astype(BF16)
        first += heads * HD


def weigh(every_ref, length_ref, hit_ref, partner_ref, chosen_ref, score_ref, loss_ref):
    row = lax.broadcasted_iota(jnp.int32, (HD, HD), 0)
    col = lax.broadcasted_iota(jnp.int32, (HD, HD), 1)
    lengths = length_ref[...]
    totals = jnp.sum(every_ref[...], axis=0, keepdims=True)
    adjusted = totals / lengths - score_ref[...]
    adjusted_col = jnp.sum(jnp.where(row == col, adjusted, 0.0), axis=1, keepdims=True)
    mate = jnp.sum(jnp.where(row == partner_ref[...], adjusted_col, 0.0), axis=0, keepdims=True)
    chosen = chosen_ref[...].astype(F32)
    sign = 2.0 * chosen - 1.0
    margin = BETA * sign * (adjusted - mate)
    softplus = jnp.maximum(-margin, 0.0) + jnp.log1p(jnp.exp(-jnp.abs(margin)))
    loss_ref[0, 0] = jnp.sum(chosen * softplus)
    weight = -sign * BETA * LOSS_SCALE / (1.0 + jnp.exp(margin)) / lengths
    return jnp.sum(hit_ref[...] * weight, axis=1, keepdims=True)


def finish(where_ref, *refs):
    small, refs = refs[:6], refs[6:]
    parts = len(HEADS)
    dq_refs, own_refs, pair_refs = (refs[i * parts : (i + 1) * parts] for i in range(3))
    near, far, out_q, out_k, out_v, loss_ref, weight_ref = refs[3 * parts :]
    step = pl.program_id(0)

    @pl.when(step == 0)
    def _():
        weight = weigh(*small, loss_ref)
        weight_ref[...] = jnp.broadcast_to(weight, weight_ref.shape)

    weight = weight_ref[...]
    even = 1.0 - lax.rem(where_ref[1], 2).astype(F32)
    origin = [(part, head) for part, heads in enumerate(HEADS) for head in range(heads)]
    for at in range(len(origin) // PER_STEP):

        @pl.when(step == at)
        def _(at=at):
            for here in range(PER_STEP):
                part, local = origin[at * PER_STEP + here]
                cols, back = cut(local, HD), cut(at * PER_STEP + here, HD)
                for out, base in ((out_k, 0), (out_v, 1)):
                    side = own_refs[part][base, :, cols]
                    side = side + even * pair_refs[part][1, base, :, cols].astype(F32)
                    side = side + near[base, :, back].astype(F32)
                    side = side + far[base, :, back].astype(F32)
                    out[:, cut(here, HD)] = (side * weight).astype(BF16)
                for g in range(GROUP):
                    dq = dq_refs[part][:, cut(local * GROUP + g, HD)].astype(F32)
                    out_q[:, cut(here * GROUP + g, HD)] = (dq * weight).astype(BF16)


def finish_all(where, small, grad_q, mines, pairs, backs):
    tok = grad_q[0].shape[0]
    steps = sum(HEADS) // PER_STEP
    arrays = [*small, *grad_q, *mines, *pairs, *backs]
    widths = [PER_STEP * GROUP * HD, PER_STEP * HD, PER_STEP * HD]
    return pl.pallas_call(
        finish,
        grid=(steps,),
        in_specs=[SMEM] + [VMEM] * len(arrays),
        out_specs=[pl.BlockSpec((tok, width), lambda i: (0, i)) for width in widths] + [SMEM],
        out_shape=[jax.ShapeDtypeStruct((tok, steps * width), BF16) for width in widths]
        + [jax.ShapeDtypeStruct((1, 1), F32)],
        scratch_shapes=[pltpu.VMEM((tok, HD), F32)],
        compiler_params=pltpu.CompilerParams(vmem_limit_bytes=VMEM_BYTES),
    )(where, *arrays)


def gather_window(own, near, far, core, halves):
    pairs = [near, jnp.where(core == 0, own, far)]
    if halves:
        half = near.shape[0] // 2
        pairs = [array[rows] for array in pairs for rows in (slice(0, half), slice(half, None))]
    pairs = [lax.ppermute(array, "ctx", SIBLING) for array in pairs]
    return (own, near, far, *pairs)


def tie(value, *others):
    return lax.optimization_barrier((value, *others))[0]


def per_device(queries, keys, values, upstream, token_logp, segments, partner, chosen, ref_score):
    place = lax.axis_index("ctx")
    where = jnp.stack([lax.axis_index("dp"), place]).astype(jnp.int32)
    core = place % 2
    tok = queries.shape[1]
    devices = lax.axis_size("dp") * CTX
    own, near, far = [], [], []
    first = 0
    for heads in HEADS:
        cols = slice(first * HD, (first + heads) * HD)
        block = jnp.concatenate([keys[0][:, cols], values[0][:, cols]], axis=1)
        own.append(block)
        near.append(lax.ppermute(block, "ctx", shift(2)))
        far.append(lax.ppermute(block, "ctx", shift(4)))
        first += heads
    parts = len(HEADS)
    bias, hit, lengths, *stacks = local_call(
        stage,
        (where, segments, queries[0], upstream[0]),
        [((WINDOW * tok, tok), F32), ((tok, HD), F32), ((1, HD), F32)]
        + [((heads * GROUP * tok, HD), BF16) for heads in HEADS] * 2,
        None,
        1,
    )

    term = token_logp
    grad_q, mines, pairs, outward = [], [], [], []
    for part, heads in enumerate(HEADS):
        final = part == len(HEADS) - 1
        ready = term if part else bias
        here, there, _ = lax.optimization_barrier((near[part], far[part], ready))
        blocks = gather_window(own[part], here, there, core, part == 0)
        term, dq, to_near, to_far, to_pair, mine = local_call(
            functools.partial(attend, heads, final),
            (where, segments, term, bias, stacks[part], stacks[parts + part], *blocks),
            [((devices, HD) if final else (1, tok), F32)] + backward_shapes(tok, heads),
            LIGHT,
            1,
        )
        grad_q.append(dq)
        mines.append(mine)
        pairs.append(lax.ppermute(to_pair, "ctx", SIBLING))
        outward += [to_near, to_far, pairs[-1]]
    shape = ((2, tok, sum(HEADS) * HD), BF16)
    near_sum, far_sum = local_call(merge, (where, *outward), [shape] * 2, LIGHT, 1)
    backs = (
        lax.ppermute(near_sum, "ctx", shift(-2)),
        lax.ppermute(far_sum, "ctx", shift(-4)),
    )

    term = tie(term, near_sum, far_sum)
    every = lax.all_to_all(term, ("dp", "ctx"), split_axis=0, concat_axis=0, tiled=True)
    small = (every, lengths, hit, partner[None], chosen[None], ref_score[None])
    out_q, out_k, out_v, loss = finish_all(where, small, grad_q, mines, pairs, backs)
    return out_q[None], out_k[None], out_v[None], loss.reshape(())


def solution(mesh):
    return jax.shard_map(
        per_device,
        mesh=mesh,
        in_specs=(
            P("dp", "ctx", None),
            P("dp", "ctx", None),
            P("dp", "ctx", None),
            P("dp", "ctx", None),
            P("dp", "ctx"),
            P(),
            P(),
            P(),
            P(),
        ),
        out_specs=(P("dp", "ctx", None), P("dp", "ctx", None), P("dp", "ctx", None), P()),
        check_vma=False,
    )
```

```python
import functools

import jax
import jax.numpy as jnp
from jax import lax
from jax.experimental import pallas as pl
from jax.experimental.pallas import tpu as pltpu
from jax.sharding import PartitionSpec as P

HD = 128
SEQS = 4
GROUP = 8
BETA = 2.0
LOSS_SCALE = 1024.0
NEG_FILL = -1e30
LOG2E = 1.4426950408889634
SCALE = HD**-0.5
WINDOW = 5
CTX = 8
VMEM_BYTES = 24 * 2**20
CHUNK = 2
HEADS = (4, 4)
PER_STEP = 4
F32 = jnp.float32
BF16 = jnp.bfloat16
NT = (((1,), (1,)), ((), ()))
TN = (((0,), (0,)), ((), ()))
VMEM = pl.BlockSpec(memory_space=pltpu.VMEM)
LIGHT = pl.CostEstimate(flops=1000, bytes_accessed=1000, transcendentals=0)
SMEM = pl.BlockSpec(memory_space=pltpu.SMEM)

SIBLING = [(i, i ^ 1) for i in range(CTX)]


def shift(by):
    return [(i, i + by) for i in range(CTX) if 0 <= i + by < CTX]


def cut(at, width):
    return slice(at * width, (at + 1) * width)


def pick_row(array, row):
    rows = lax.broadcasted_iota(jnp.int32, array.shape, 0)
    return jnp.sum(jnp.where(rows == row, array, 0), axis=0, keepdims=True)


def window_bias(rank, place, seg_ref, tok):
    pack = pick_row(seg_ref[...], rank)
    mine = pick_row(seg_ref[:, pl.ds(pl.multiple_of(place * tok, tok), tok)], rank)
    start = jnp.zeros((1, tok), jnp.int32)
    for slot in range(SEQS - 1):
        count = jnp.sum((pack == slot).astype(F32)).astype(jnp.int32)
        start = start + jnp.where(mine > slot, count, 0)
    last = place * tok + lax.broadcasted_iota(jnp.int32, (1, tok), 1)
    core = lax.rem(place, 2)
    at = lax.broadcasted_iota(jnp.int32, (tok, tok), 0)
    parts = []
    for block in (place, place - 2, place - 4, place - 1 - 2 * core, place - 3 + 2 * core):
        pos = at + block * tok
        parts.append(jnp.where((pos >= start) & (pos <= last), 0.0, NEG_FILL))
    return jnp.concatenate(parts, axis=0), mine


def lengths_row(seg):
    packs = seg.shape[0]
    lane = lax.broadcasted_iota(jnp.int32, (1, HD), 1)
    counts = jnp.zeros((packs, HD), F32)
    for slot in range(SEQS):
        count = jnp.sum((seg == slot).astype(F32), axis=1, keepdims=True)
        counts = counts + jnp.where(lax.rem(lane, SEQS) == slot, count, 0.0)
    pack_of = lax.broadcasted_iota(jnp.int32, (packs, HD), 0) * SEQS
    held = (lane >= pack_of) & (lane < pack_of + SEQS)
    return jnp.sum(jnp.where(held, counts, 0.0), axis=0, keepdims=True)


def stage(where_ref, seg_ref, q_ref, u_ref, bias_ref, hit_ref, length_ref, *stacks):
    tok = q_ref.shape[0]
    rank = where_ref[0]
    bias_ref[...], mine = window_bias(rank, where_ref[1], seg_ref, tok)
    length_ref[...] = lengths_row(seg_ref[...])
    row = lax.broadcasted_iota(jnp.int32, (tok, HD), 0)
    col = lax.broadcasted_iota(jnp.int32, (tok, HD), 1)
    mine = jnp.sum(jnp.where(row == col, mine.astype(F32), 0.0), axis=1, keepdims=True)
    hit_ref[...] = (col == mine.astype(jnp.int32) + rank * SEQS).astype(F32)
    parts = len(HEADS)
    for source, outs in ((q_ref, stacks[:parts]), (u_ref, stacks[parts:])):
        first = 0
        for out, heads in zip(outs, HEADS):
            for g in range(heads * GROUP):
                out[cut(g, tok), :] = source[:, cut(first + g, HD)]
            first += heads * GROUP


def window(blocks, head):
    return jnp.concatenate([ref[:, cut(head, HD)] for ref in blocks], axis=0)


def forward_chunk(keys, values, q, u, bias):
    scores = lax.dot_general(keys, q, NT, preferred_element_type=F32)
    scores = scores * (SCALE * LOG2E) + bias
    expo = jnp.exp2(scores - jnp.max(scores, axis=0, keepdims=True))
    share = 1.0 / jnp.sum(expo, axis=0, keepdims=True)
    probs = expo.astype(BF16) * share.astype(BF16)
    dprob = lax.dot_general(values, u, NT, preferred_element_type=F32)
    delta = jnp.sum(expo * dprob, axis=0, keepdims=True) * share
    return probs, probs * (dprob - delta).astype(BF16), delta


def forward_head(keys, values, q, u, bias):
    chunks = []
    for at in range(GROUP // CHUNK):
        rows = cut(at, q.shape[0] // (GROUP // CHUNK))
        chunks.append(forward_chunk(keys, values, q[rows], u[rows], bias))
    return (jnp.concatenate(side, axis=1) for side in zip(*chunks))


def backward_head(head, keys, q, u, probs, dscore, outs):
    dq_ref, near_ref, far_ref, pair_ref, own_ref = outs
    tok = near_ref.shape[1]
    dv = jnp.dot(probs, u, preferred_element_type=F32)
    dk = jnp.dot(dscore, q, preferred_element_type=F32)
    dq = lax.dot_general(dscore, keys, TN, preferred_element_type=F32)
    for g in range(GROUP):
        dq_ref[:, cut(head * GROUP + g, HD)] = dq[cut(g, tok)].astype(BF16)
    cols = cut(head, HD)
    for side, part in enumerate((dk, dv)):
        own_ref[side, :, cols] = part[:tok]
        near_ref[side, :, cols] = part[cut(1, tok)].astype(BF16)
        far_ref[side, :, cols] = part[cut(2, tok)].astype(BF16)
        pair_ref[0, side, :, cols] = part[cut(3, tok)].astype(BF16)
        pair_ref[1, side, :, cols] = part[cut(4, tok)].astype(BF16)


def backward_shapes(tok, heads):
    width = heads * HD
    return [
        ((tok, heads * GROUP * HD), BF16),
        ((2, tok, width), BF16),
        ((2, tok, width), BF16),
        ((2, 2, tok, width), BF16),
        ((2, tok, width), F32),
    ]


def local_call(kernel, args, shapes, cost, scalars=0):
    return pl.pallas_call(
        kernel,
        in_specs=[SMEM] * scalars + [VMEM] * (len(args) - scalars),
        out_specs=[VMEM] * len(shapes),
        out_shape=[jax.ShapeDtypeStruct(shape, dtype) for shape, dtype in shapes],
        compiler_params=pltpu.CompilerParams(vmem_limit_bytes=VMEM_BYTES),
        cost_estimate=cost,
    )(*args)


def attend(heads, final, where_ref, seg_ref, term_in, bias_ref, q_ref, u_ref, *refs):
    blocks, term_ref, outs = refs[:-6], refs[-6], refs[-5:]
    tok = bias_ref.shape[1]
    bias = jnp.concatenate([bias_ref[...]] * CHUNK, axis=1)
    term = term_in[...]
    for head in range(heads):
        keys, values = window(blocks, head), window(blocks, heads + head)
        rows = cut(head, GROUP * tok)
        q, u = q_ref[rows, :], u_ref[rows, :]
        probs, dscore, delta = forward_head(keys, values, q, u, bias)
        for g in range(GROUP):
            term = term + delta[:, cut(g, tok)]
        backward_head(head, keys, q, u, probs, dscore, outs)
    if final:
        rank, place = where_ref[0], where_ref[1]
        mine = pick_row(seg_ref[:, pl.ds(pl.multiple_of(place * tok, tok), tok)], rank)
        lane = lax.broadcasted_iota(jnp.int32, (1, HD), 1)
        row = jnp.zeros((1, HD), F32)
        for slot in range(SEQS):
            total = jnp.sum(jnp.where(mine == slot, term, 0.0), axis=1, keepdims=True)
            row = row + jnp.where(lane == rank * SEQS + slot, total, 0.0)
        term_ref[...] = jnp.broadcast_to(row, term_ref.shape)
    else:
        term_ref[...] = term


def merge(where_ref, *refs):
    near_out, far_out = refs[-2:]
    core = lax.rem(where_ref[1], 2).astype(F32)
    first = 0
    for part, heads in enumerate(HEADS):
        near, far, pair = refs[3 * part : 3 * part + 3]
        cols = slice(first, first + heads * HD)
        near_out[:, :, cols] = (near[...].astype(F32) + pair[0].astype(F32)).astype(BF16)
        far_out[:, :, cols] = (far[...].astype(F32) + core * pair[1].astype(F32)).astype(BF16)
        first += heads * HD


def weigh(every_ref, length_ref, hit_ref, partner_ref, chosen_ref, score_ref, loss_ref):
    row = lax.broadcasted_iota(jnp.int32, (HD, HD), 0)
    col = lax.broadcasted_iota(jnp.int32, (HD, HD), 1)
    lengths = length_ref[...]
    totals = jnp.sum(every_ref[...], axis=0, keepdims=True)
    adjusted = totals / lengths - score_ref[...]
    adjusted_col = jnp.sum(jnp.where(row == col, adjusted, 0.0), axis=1, keepdims=True)
    mate = jnp.sum(jnp.where(row == partner_ref[...], adjusted_col, 0.0), axis=0, keepdims=True)
    chosen = chosen_ref[...].astype(F32)
    sign = 2.0 * chosen - 1.0
    margin = BETA * sign * (adjusted - mate)
    softplus = jnp.maximum(-margin, 0.0) + jnp.log1p(jnp.exp(-jnp.abs(margin)))
    loss_ref[0, 0] = jnp.sum(chosen * softplus)
    weight = -sign * BETA * LOSS_SCALE / (1.0 + jnp.exp(margin)) / lengths
    return jnp.sum(hit_ref[...] * weight, axis=1, keepdims=True)


def finish(where_ref, *refs):
    small, refs = refs[:6], refs[6:]
    parts = len(HEADS)
    dq_refs, own_refs, pair_refs = (refs[i * parts : (i + 1) * parts] for i in range(3))
    near, far, out_q, out_k, out_v, loss_ref, weight_ref = refs[3 * parts :]
    step = pl.program_id(0)

    @pl.when(step == 0)
    def _():
        weight = weigh(*small, loss_ref)
        weight_ref[...] = jnp.broadcast_to(weight, weight_ref.shape)

    weight = weight_ref[...]
    scaled = weight * SCALE
    even = 1.0 - lax.rem(where_ref[1], 2).astype(F32)
    origin = [(part, head) for part, heads in enumerate(HEADS) for head in range(heads)]
    for at in range(len(origin) // PER_STEP):

        @pl.when(step == at)
        def _(at=at):
            for here in range(PER_STEP):
                part, local = origin[at * PER_STEP + here]
                cols, back = cut(local, HD), cut(at * PER_STEP + here, HD)
                for out, base, factor in ((out_k, 0, scaled), (out_v, 1, weight)):
                    side = own_refs[part][base, :, cols]
                    side = side + even * pair_refs[part][1, base, :, cols].astype(F32)
                    side = side + near[base, :, back].astype(F32)
                    side = side + far[base, :, back].astype(F32)
                    out[:, cut(here, HD)] = (side * factor).astype(BF16)
                for g in range(GROUP):
                    dq = dq_refs[part][:, cut(local * GROUP + g, HD)].astype(F32)
                    out_q[:, cut(here * GROUP + g, HD)] = (dq * scaled).astype(BF16)


def finish_all(where, small, grad_q, mines, pairs, backs):
    tok = grad_q[0].shape[0]
    steps = sum(HEADS) // PER_STEP
    arrays = [*small, *grad_q, *mines, *pairs, *backs]
    widths = [PER_STEP * GROUP * HD, PER_STEP * HD, PER_STEP * HD]
    return pl.pallas_call(
        finish,
        grid=(steps,),
        in_specs=[SMEM] + [VMEM] * len(arrays),
        out_specs=[pl.BlockSpec((tok, width), lambda i: (0, i)) for width in widths] + [SMEM],
        out_shape=[jax.ShapeDtypeStruct((tok, steps * width), BF16) for width in widths]
        + [jax.ShapeDtypeStruct((1, 1), F32)],
        scratch_shapes=[pltpu.VMEM((tok, HD), F32)],
        compiler_params=pltpu.CompilerParams(vmem_limit_bytes=VMEM_BYTES),
    )(where, *arrays)


def gather_window(own, near, far, core, halves):
    pairs = [near, jnp.where(core == 0, own, far)]
    if halves:
        half = near.shape[0] // 2
        pairs = [array[rows] for array in pairs for rows in (slice(0, half), slice(half, None))]
    pairs = [lax.ppermute(array, "ctx", SIBLING) for array in pairs]
    return (own, near, far, *pairs)


def tie(value, *others):
    return lax.optimization_barrier((value, *others))[0]


def per_device(queries, keys, values, upstream, token_logp, segments, partner, chosen, ref_score):
    place = lax.axis_index("ctx")
    where = jnp.stack([lax.axis_index("dp"), place]).astype(jnp.int32)
    core = place % 2
    tok = queries.shape[1]
    devices = lax.axis_size("dp") * CTX
    own, near, far = [], [], []
    first = 0
    for heads in HEADS:
        cols = slice(first * HD, (first + heads) * HD)
        block = jnp.concatenate([keys[0][:, cols], values[0][:, cols]], axis=1)
        own.append(block)
        near.append(lax.ppermute(block, "ctx", shift(2)))
        far.append(lax.ppermute(block, "ctx", shift(4)))
        first += heads
    parts = len(HEADS)
    bias, hit, lengths, *stacks = local_call(
        stage,
        (where, segments, queries[0], upstream[0]),
        [((WINDOW * tok, tok), F32), ((tok, HD), F32), ((1, HD), F32)]
        + [((heads * GROUP * tok, HD), BF16) for heads in HEADS] * 2,
        None,
        1,
    )

    term = token_logp
    grad_q, mines, pairs, outward = [], [], [], []
    for part, heads in enumerate(HEADS):
        final = part == len(HEADS) - 1
        ready = term if part else bias
        here, there, _ = lax.optimization_barrier((near[part], far[part], ready))
        blocks = gather_window(own[part], here, there, core, part == 0)
        term, dq, to_near, to_far, to_pair, mine = local_call(
            functools.partial(attend, heads, final),
            (where, segments, term, bias, stacks[part], stacks[parts + part], *blocks),
            [((devices, HD) if final else (1, tok), F32)] + backward_shapes(tok, heads),
            LIGHT,
            1,
        )
        grad_q.append(dq)
        mines.append(mine)
        pairs.append(lax.ppermute(to_pair, "ctx", SIBLING))
        outward += [to_near, to_far, pairs[-1]]
    shape = ((2, tok, sum(HEADS) * HD), BF16)
    near_sum, far_sum = local_call(merge, (where, *outward), [shape] * 2, LIGHT, 1)
    backs = (
        lax.ppermute(near_sum, "ctx", shift(-2)),
        lax.ppermute(far_sum, "ctx", shift(-4)),
    )

    term = tie(term, near_sum, far_sum)
    every = lax.all_to_all(term, ("dp", "ctx"), split_axis=0, concat_axis=0, tiled=True)
    small = (every, lengths, hit, partner[None], chosen[None], ref_score[None])
    out_q, out_k, out_v, loss = finish_all(where, small, grad_q, mines, pairs, backs)
    return out_q[None], out_k[None], out_v[None], loss.reshape(())


def solution(mesh):
    return jax.shard_map(
        per_device,
        mesh=mesh,
        in_specs=(
            P("dp", "ctx", None),
            P("dp", "ctx", None),
            P("dp", "ctx", None),
            P("dp", "ctx", None),
            P("dp", "ctx"),
            P(),
            P(),
            P(),
            P(),
        ),
        out_specs=(P("dp", "ctx", None), P("dp", "ctx", None), P("dp", "ctx", None), P()),
        check_vma=False,
    )
```
